32 devices in a mesh: lon: 16 (over z, y, core), plane: 2 (over x).
Axes of the slice: x: 2, y: 2, z: 4, core: 2. Of those that a mesh axis runs over, the one named last changes fastest.
Arguments:
- potential: float32 [2, 256, 4096], P('plane', None, 'lon'), may hold values from -0.6 to 0.6
- lens_weight: float32 [2, 2], P('plane'), may hold values from 0.1 to 0.3
- cycle_shift: int32 [2, 256], replicated, may hold values from -3 to 2
- cycle_weight: int32 [2, 256], replicated, may hold values from 0 to 16
- cycle_scale: float32 [256], replicated, may hold values from 1 to 2
Outputs:
- displacement: float32 [2, 2, 256, 4096], P('plane', None, None, 'lon')
- jacobian: float32 [2, 4, 256, 4096], P('plane', None, None, 'lon')
The draws below stay inside these ranges and needn't reach their ends.
All inputs are finite; a program needn't handle non-finite values.
Results may differ from the reference program's by a relative error of at most 0.00002.
Values sent between devices are 32-bit elements; how exact they have to be, the bound alone decides.
A program may use at most 64 MiB of HBM per device.

```python
import math
import jax
import jax.numpy as jnp
from jax import lax

ROWS = 256
NLON = 4096
PLANES = 2
SOURCES = 2


def set_ends(array, key, least, largest):
    shape = array.shape
    index_at = [jax.random.randint(jax.random.fold_in(key, axis), (), 0, shape[axis]) for axis in range(len(shape))]
    array = array.at[tuple(index_at)].set(least)
    longest = shape.index(max(shape))
    index_at[longest] = (index_at[longest] + 1) % shape[longest]
    return array.at[tuple(index_at)].set(largest)


def block_scale(own_key, shape, shards, smallest, high):
    level, own = 1.0, jax.random.fold_in(own_key, 6)
    for axis_at, blocks in shards:
        heights = jnp.exp(jax.random.uniform(jax.random.fold_in(own, axis_at), (blocks,), jnp.float32, smallest / len(shards), high / len(shards)))
        level = level * jnp.repeat(heights, shape[axis_at] // blocks).reshape([-1 if axis == axis_at else 1 for axis in range(len(shape))])
    return level


def gaussian(key, dims, deviation, bound, split=(), kind=jnp.bfloat16):
    loudness = block_scale(key, dims, split, -0.22, 0.18) if split else 1.0
    values = jax.random.normal(key, dims, jnp.float32) * deviation * loudness
    return jnp.minimum(jnp.maximum(values, -bound), bound).astype(kind)


def setup_inputs(seed: int = 0) -> dict:
    streams_of = jax.random.split(jax.random.key(seed), 6)
    potential = gaussian(streams_of[0], (PLANES, ROWS, NLON), 0.1, 0.6, ((0, 2), (2, 16)), jnp.float32)
    lens_weight = jnp.clip(0.1 + 0.20000001043081284 * jax.random.uniform(streams_of[1], (SOURCES, PLANES), jnp.float32) ** block_scale(streams_of[1], (SOURCES, PLANES), ((0, 2),), -0.2, 0.2), 0.1, 0.3)
    cycle_shift = set_ends(jax.random.randint(streams_of[2], (2, ROWS), -3, 3), jax.random.fold_in(streams_of[2], 1), -3, 2).astype(jnp.int32)
    cycle_weight = set_ends(jax.random.randint(streams_of[3], (2, ROWS), 0, 17), jax.random.fold_in(streams_of[3], 1), 0, 16).astype(jnp.int32)
    cycle_scale = jnp.clip(jnp.exp(jax.random.uniform(streams_of[4], (ROWS,), jnp.float32, math.log(1.0), math.log(2.0))), 1.0, 2.0)
    return {"potential": potential, "lens_weight": lens_weight, "cycle_shift": cycle_shift, "cycle_weight": cycle_weight, "cycle_scale": cycle_scale}


def cycle_interp(row_block, shifts, weights, offset, total):
    columns = jnp.arange(total, dtype=jnp.int32)
    index = (columns[None, :] + shifts[:, None].astype(jnp.int32) + offset) % total
    picked = jnp.take_along_axis(row_block, index, axis=1)
    index_next = (index + 1) % total
    picked_next = jnp.take_along_axis(row_block, index_next, axis=1)
    frac = weights.astype(jnp.float32)[:, None] / 16.0
    return (1.0 - frac) * picked + frac * picked_next


def derivatives(field, cycle_shift, cycle_weight, cycle_scale):
    total = field.shape[1]
    padded = jnp.pad(field, ((1, 1), (0, 0)))
    north_rows = padded[:-2]
    south_rows = padded[2:]
    north = [cycle_interp(north_rows, cycle_shift[0], cycle_weight[0], offset, total) for offset in (-1, 0, 1)]
    south = [cycle_interp(south_rows, cycle_shift[1], cycle_weight[1], offset, total) for offset in (-1, 0, 1)]
    center = [jnp.roll(field, -offset, axis=1) for offset in (-1, 0, 1)]
    metric = cycle_scale[:, None]
    alpha_t = 0.5 * (south[1] - north[1])
    alpha_p = 0.5 * metric * (center[2] - center[0])
    shear_tt = south[1] - 2.0 * center[1] + north[1]
    shear_pp = metric * metric * (center[2] - 2.0 * center[1] + center[0])
    shear_tp = 0.25 * metric * (south[2] - south[0] - north[2] + north[0])
    return alpha_t, alpha_p, shear_tt, shear_pp, shear_tp


def advance(state, fields, gain):
    disp_t, disp_p, a_zz, a_zo, a_oz, a_oo = state
    alpha_t, alpha_p, shear_tt, shear_pp, shear_tp = fields
    new_t = disp_t - gain * (alpha_t + shear_tt * disp_t + shear_tp * disp_p)
    new_p = disp_p - gain * (alpha_p + shear_tp * disp_t + shear_pp * disp_p)
    b_zz = a_zz - gain * (shear_tt * a_zz + shear_tp * a_oz)
    b_zo = a_zo - gain * (shear_tt * a_zo + shear_tp * a_oo)
    b_oz = a_oz - gain * (shear_tp * a_zz + shear_pp * a_oz)
    b_oo = a_oo - gain * (shear_tp * a_zo + shear_pp * a_oo)
    return (new_t, new_p, b_zz, b_zo, b_oz, b_oo)


def reference(potential, lens_weight, cycle_shift, cycle_weight, cycle_scale):
    turn = NLON // 4
    skies = [jnp.roll(potential[plane_k], -turn, axis=1) for plane_k in range(PLANES)]

    def one_source(gains):
        zeros = jnp.zeros((ROWS, NLON), jnp.float32)
        ones = jnp.ones((ROWS, NLON), jnp.float32)
        state = (zeros, zeros, ones, zeros, zeros, ones)
        for plane_k in range(PLANES):
            fields = derivatives(skies[plane_k], cycle_shift, cycle_weight, cycle_scale)
            state = advance(state, fields, gains[plane_k])
        return jnp.stack(state)

    result = lax.map(one_source, lens_weight)
    return result[:, 0:2], result[:, 2:6]
```

```python
import functools

import jax
import jax.numpy as jnp
from jax import lax
from jax.experimental import pallas as pl
from jax.experimental.pallas import tpu as pltpu
from jax.sharding import PartitionSpec as P

LANES = 128
PACK = 8
CHUNKS = 8
GROUP = 16


def exchange_kernel(
    planes, count, turn,
    pot, shift, weight, scale,
    sky, halo, params,
    tile, low_pack, high_pack, strips, columns,
    load_sem, turn_send, turn_recv, plane_send, plane_recv, halo_send, halo_recv,
):
    me = lax.axis_index("lon")
    own = lax.axis_index("plane")
    rows = pot.shape[1]
    step = rows // CHUNKS

    def at(moves, plane):
        return {"lon": lax.rem(me + moves + count, count), "plane": plane}

    others = [lax.rem(own + d, planes) for d in range(1, planes)]
    load = pltpu.make_async_copy(pot.at[0], tile, load_sem)
    load.start()

    barrier = pltpu.get_barrier_semaphore()
    senders = [at(turn, own)] + [at(0, q) for q in others]
    senders += [at(turn + side, q) for side in (-1, 1) for q in [own] + others]
    for device in senders:
        pl.semaphore_signal(
            barrier, inc=1, device_id=device, device_id_type=pl.DeviceIdType.MESH
        )
    pl.semaphore_wait(barrier, len(senders))

    turned = []
    for k in range(CHUNKS):
        part = pl.ds(k * step, step)
        copy = pltpu.make_async_remote_copy(
            src_ref=pot.at[0, part],
            dst_ref=sky.at[own, part],
            send_sem=turn_send.at[k],
            recv_sem=turn_recv.at[k],
            device_id=at(-turn, own),
            device_id_type=pl.DeviceIdType.MESH,
        )
        copy.start()
        turned.append(copy)

    load.wait()
    low_pack[...] = jnp.transpose(tile[:, :LANES])[:PACK]
    high_pack[...] = jnp.transpose(tile[:, tile.shape[1] - LANES :])[LANES - PACK :]
    edges = []
    for i, q in enumerate([own] + others):
        for side, (source, first, moves) in enumerate(
            ((low_pack, 0, -turn - 1), (high_pack, LANES - PACK, -turn + 1))
        ):
            copy = pltpu.make_async_remote_copy(
                src_ref=source,
                dst_ref=strips.at[own, pl.ds(first, PACK)],
                send_sem=halo_send.at[i, side],
                recv_sem=halo_recv.at[own, side],
                device_id=at(moves, q),
                device_id_type=pl.DeviceIdType.MESH,
            )
            copy.start()
            edges.append(copy)

    columns[...] = jnp.zeros_like(columns)
    columns[0:2] = shift[...].astype(jnp.float32)
    columns[2:4] = weight[...].astype(jnp.float32) / 16.0
    columns[4:5] = scale[...].reshape(1, rows)
    params[...] = jnp.transpose(columns[...])
    strips[:, PACK : LANES - PACK] = jnp.zeros(
        (planes, LANES - 2 * PACK, rows), jnp.float32
    )

    handed = []
    for k in range(CHUNKS):
        part = pl.ds(k * step, step)
        turned[k].wait_recv()
        for i, q in enumerate(others):
            copy = pltpu.make_async_remote_copy(
                src_ref=sky.at[own, part],
                dst_ref=sky.at[own, part],
                send_sem=plane_send.at[i, k],
                recv_sem=plane_recv.at[own, k],
                device_id=at(0, q),
                device_id_type=pl.DeviceIdType.MESH,
            )
            copy.start()
            handed.append(copy)

    for q in [own] + others:
        for side, (source, first) in enumerate(((low_pack, 0), (high_pack, LANES - PACK))):
            pltpu.make_async_remote_copy(
                src_ref=source,
                dst_ref=strips.at[q, pl.ds(first, PACK)],
                send_sem=halo_send.at[0, side],
                recv_sem=halo_recv.at[q, side],
                device_id=at(0, others[0]),
                device_id_type=pl.DeviceIdType.MESH,
            ).wait_recv()
    for k in range(planes):
        halo[k] = jnp.transpose(strips[k])

    for q in others:
        for k in range(CHUNKS):
            part = pl.ds(k * step, step)
            pltpu.make_async_remote_copy(
                src_ref=sky.at[q, part],
                dst_ref=sky.at[q, part],
                send_sem=plane_send.at[0, k],
                recv_sem=plane_recv.at[q, k],
                device_id=at(0, others[0]),
                device_id_type=pl.DeviceIdType.MESH,
            ).wait_recv()
    for copy in turned + edges + handed:
        copy.wait_send()


def ray_kernel(planes, gains, sky, halo, params, disp, jac, disp_buf, jac_buf, out_sem):
    rows = sky.shape[1]
    blocks = sky.shape[2] // LANES
    total = blocks + 1
    lane = lax.broadcasted_iota(jnp.int32, (GROUP, LANES), 1)
    row = lax.broadcasted_iota(jnp.int32, (GROUP, LANES), 0)

    def right(parts):
        turned = [pltpu.roll(part, LANES - 1, 1) for part in parts]
        return [
            jnp.where(lane == LANES - 1, turned[(v + 1) % total], turned[v])
            for v in range(total)
        ]

    def left(parts):
        turned = [pltpu.roll(part, 1, 1) for part in parts]
        return [jnp.where(lane == 0, turned[v - 1], turned[v]) for v in range(total)]

    def load(k, start, stop):
        parts = [sky[k, start:stop, v * LANES : (v + 1) * LANES] for v in range(blocks)]
        return parts + [halo[k, start:stop, :]]

    copies = []
    for g in range(rows // GROUP):
        start, stop = g * GROUP, (g + 1) * GROUP
        column = [
            jnp.broadcast_to(params[start:stop, i : i + 1], (GROUP, LANES)) for i in range(5)
        ]
        metric = column[4]
        stencils = []
        for side in range(2):
            place = lane + column[side].astype(jnp.int32)
            frac = column[2 + side]
            stencils.append((place & (LANES - 1), place < 0, place >= LANES, frac, 1.0 - frac))
        state = [None] * blocks
        for k in range(planes):
            gain = gains[0, k]
            here = load(k, start, stop)
            if g == 0:
                above = [jnp.where(row == 0, 0.0, pltpu.roll(part, 1, 0)) for part in here]
            else:
                above = load(k, start - 1, stop - 1)
            if stop == rows:
                below = [
                    jnp.where(row == GROUP - 1, 0.0, pltpu.roll(part, GROUP - 1, 0))
                    for part in here
                ]
            else:
                below = load(k, start + 1, stop + 1)
            values = []
            for (place, under, over, frac, rest), parts in zip(stencils, (above, below)):
                mixed = [rest * a + frac * b for a, b in zip(parts, right(parts))]
                picked = [jnp.take_along_axis(part, place, axis=1) for part in mixed]
                values.append(
                    [
                        jnp.where(
                            under,
                            picked[v - 1],
                            jnp.where(over, picked[(v + 1) % total], picked[v]),
                        )
                        for v in range(total)
                    ]
                )
            north, south = values
            slope = [s - n for s, n in zip(south, north)]
            slope_right, slope_left = right(slope), left(slope)
            here_right, here_left = right(here), left(here)
            for v in range(blocks):
                alpha_t = 0.5 * slope[v]
                alpha_p = 0.5 * metric * (here_right[v] - here_left[v])
                u_tt = south[v] - 2.0 * here[v] + north[v]
                u_pp = metric * metric * (here_right[v] - 2.0 * here[v] + here_left[v])
                u_tp = 0.25 * metric * (slope_right[v] - slope_left[v])
                if k == 0:
                    off = -gain * u_tp
                    state[v] = (
                        -gain * alpha_t, -gain * alpha_p,
                        1.0 - gain * u_tt, off, off, 1.0 - gain * u_pp,
                    )
                else:
                    d_t, d_p, zz, zo, oz, oo = state[v]
                    state[v] = (
                        d_t - gain * (alpha_t + u_tt * d_t + u_tp * d_p),
                        d_p - gain * (alpha_p + u_tp * d_t + u_pp * d_p),
                        zz - gain * (u_tt * zz + u_tp * oz),
                        zo - gain * (u_tt * zo + u_tp * oo),
                        oz - gain * (u_tp * zz + u_pp * oz),
                        oo - gain * (u_tp * zo + u_pp * oo),
                    )
        for v in range(blocks):
            part = pl.ds(v * LANES, LANES)
            for i in range(2):
                disp_buf[i, start:stop, part] = state[v][i]
            for i in range(4):
                jac_buf[i, start:stop, part] = state[v][2 + i]
        here = pl.ds(start, GROUP)
        for i, (source, target) in enumerate(((disp_buf, disp), (jac_buf, jac))):
            copy = pltpu.make_async_copy(
                source.at[:, here], target.at[0, :, here], out_sem.at[i, g]
            )
            copy.start()
            copies.append(copy)
    for copy in copies:
        copy.wait()


def per_device(planes, count, potential, lens_weight, cycle_shift, cycle_weight, cycle_scale):
    rows, width = potential.shape[1:]
    f32 = jnp.float32
    vmem = pl.BlockSpec(memory_space=pltpu.VMEM)
    anywhere = pl.BlockSpec(memory_space=pl.ANY)
    dma = pltpu.SemaphoreType.DMA
    sky, halo, params = pl.pallas_call(
        functools.partial(exchange_kernel, planes, count, count // 4),
        out_shape=(
            jax.ShapeDtypeStruct((planes, rows, width), f32),
            jax.ShapeDtypeStruct((planes, rows, LANES), f32),
            jax.ShapeDtypeStruct((rows, LANES), f32),
        ),
        in_specs=[anywhere, vmem, vmem, vmem],
        out_specs=(vmem, vmem, vmem),
        scratch_shapes=[
            pltpu.VMEM((rows, width), f32),
            pltpu.VMEM((PACK, rows), f32),
            pltpu.VMEM((PACK, rows), f32),
            pltpu.VMEM((planes, LANES, rows), f32),
            pltpu.VMEM((LANES, rows), f32),
            dma,
            dma((CHUNKS,)),
            dma((CHUNKS,)),
            dma((planes - 1, CHUNKS)),
            dma((planes, CHUNKS)),
            dma((planes, 2)),
            dma((planes, 2)),
        ],
        compiler_params=pltpu.CompilerParams(
            collective_id=0, has_side_effects=True, vmem_limit_bytes=32 * 2**20
        ),
        name="exchange",
    )(potential, cycle_shift, cycle_weight, cycle_scale)
    return tuple(
        pl.pallas_call(
            functools.partial(ray_kernel, planes),
            out_shape=(
                jax.ShapeDtypeStruct((1, 2, rows, width), f32),
                jax.ShapeDtypeStruct((1, 4, rows, width), f32),
            ),
            in_specs=[pl.BlockSpec(memory_space=pltpu.SMEM), vmem, vmem, vmem],
            out_specs=(anywhere, anywhere),
            scratch_shapes=[
                pltpu.VMEM((2, rows, width), f32),
                pltpu.VMEM((4, rows, width), f32),
                dma((2, rows // GROUP)),
            ],
            compiler_params=pltpu.CompilerParams(vmem_limit_bytes=32 * 2**20),
            name="rays",
        )(lens_weight, sky, halo, params)
    )


def solution(mesh):
    in_specs = (P("plane", None, "lon"), P("plane", None), P(), P(), P())
    out_specs = (P("plane", None, None, "lon"), P("plane", None, None, "lon"))
    return jax.shard_map(
        functools.partial(per_device, mesh.shape["plane"], mesh.shape["lon"]),
        mesh=mesh, in_specs=in_specs, out_specs=out_specs, check_vma=False,
    )
```

```python
import functools

import jax
import jax.numpy as jnp
from jax import lax
from jax.experimental import pallas as pl
from jax.experimental.pallas import tpu as pltpu
from jax.sharding import PartitionSpec as P

LANES = 128
PACK = 8
CHUNKS = 8
GROUP = 32
WINDOW = 3


def exchange_kernel(
    planes, count, turn,
    pot, gains_hbm, shift_hbm, weight_hbm, scale_hbm,
    sky, halo, params,
    tile, gains, shift, weight, scale, low_pack, high_pack, strips, columns,
    load_sem, turn_send, turn_recv, plane_send, plane_recv, halo_send, halo_recv,
):
    me = lax.axis_index("lon")
    own = lax.axis_index("plane")
    rows = pot.shape[1]
    step = rows // CHUNKS

    def at(moves, plane):
        return {"lon": lax.rem(me + moves + count, count), "plane": plane}

    others = [lax.rem(own + d, planes) for d in range(1, planes)]
    loads = [
        pltpu.make_async_copy(source, target, load_sem.at[i])
        for i, (source, target) in enumerate(
            (
                (pot.at[0], tile), (gains_hbm, gains), (shift_hbm, shift),
                (weight_hbm, weight), (scale_hbm, scale),
            )
        )
    ]
    for load in loads:
        load.start()

    barrier = pltpu.get_barrier_semaphore()
    senders = [at(turn, own)] + [at(0, q) for q in others]
    senders += [at(turn + side, q) for side in (-1, 1) for q in [own] + others]
    for device in senders:
        pl.semaphore_signal(
            barrier, inc=1, device_id=device, device_id_type=pl.DeviceIdType.MESH
        )
    pl.semaphore_wait(barrier, len(senders))

    turned = []
    for k in range(CHUNKS):
        part = pl.ds(k * step, step)
        copy = pltpu.make_async_remote_copy(
            src_ref=pot.at[0, part],
            dst_ref=sky.at[own, part],
            send_sem=turn_send.at[k],
            recv_sem=turn_recv.at[k],
            device_id=at(-turn, own),
            device_id_type=pl.DeviceIdType.MESH,
        )
        turned.append(copy)
    for copy in turned[:WINDOW]:
        copy.start()

    for load in loads:
        load.wait()
    low_pack[...] = jnp.transpose(tile[:, :LANES])[:PACK]
    high_pack[...] = jnp.transpose(tile[:, tile.shape[1] - LANES :])[LANES - PACK :]
    edges = []
    for i, q in enumerate([own] + others):
        for side, (source, first, moves) in enumerate(
            ((low_pack, 0, -turn - 1), (high_pack, LANES - PACK, -turn + 1))
        ):
            copy = pltpu.make_async_remote_copy(
                src_ref=source,
                dst_ref=strips.at[own, pl.ds(first, PACK)],
                send_sem=halo_send.at[i, side],
                recv_sem=halo_recv.at[own, side],
                device_id=at(moves, q),
                device_id_type=pl.DeviceIdType.MESH,
            )
            copy.start()
            edges.append(copy)

    columns[...] = jnp.zeros_like(columns)
    columns[0:2] = shift[...].astype(jnp.float32)
    columns[2:4] = weight[...].astype(jnp.float32) / 16.0
    columns[4:5] = scale[...].reshape(1, rows)
    for k in range(planes):
        columns[5 + k : 6 + k] = jnp.full((1, rows), gains[0, k], jnp.float32)
    params[...] = jnp.transpose(columns[...])
    strips[:, PACK : LANES - PACK] = jnp.zeros(
        (planes, LANES - 2 * PACK, rows), jnp.float32
    )

    handed = []
    for k in range(CHUNKS):
        part = pl.ds(k * step, step)
        if k + WINDOW < CHUNKS:
            turned[k].wait_send()
            turned[k + WINDOW].start()
        turned[k].wait_recv()
        for i, q in enumerate(others):
            copy = pltpu.make_async_remote_copy(
                src_ref=sky.at[own, part],
                dst_ref=sky.at[own, part],
                send_sem=plane_send.at[i, k],
                recv_sem=plane_recv.at[own, k],
                device_id=at(0, q),
                device_id_type=pl.DeviceIdType.MESH,
            )
            copy.start()
            handed.append(copy)

    for q in [own] + others:
        for side, (source, first) in enumerate(((low_pack, 0), (high_pack, LANES - PACK))):
            pltpu.make_async_remote_copy(
                src_ref=source,
                dst_ref=strips.at[q, pl.ds(first, PACK)],
                send_sem=halo_send.at[0, side],
                recv_sem=halo_recv.at[q, side],
                device_id=at(0, others[0]),
                device_id_type=pl.DeviceIdType.MESH,
            ).wait_recv()
    for k in range(planes):
        halo[k] = jnp.transpose(strips[k])

    for q in others:
        for k in range(CHUNKS):
            part = pl.ds(k * step, step)
            pltpu.make_async_remote_copy(
                src_ref=sky.at[q, part],
                dst_ref=sky.at[q, part],
                send_sem=plane_send.at[0, k],
                recv_sem=plane_recv.at[q, k],
                device_id=at(0, others[0]),
                device_id_type=pl.DeviceIdType.MESH,
            ).wait_recv()
    for copy in turned[CHUNKS - WINDOW :] + edges + handed:
        copy.wait_send()


def ray_kernel(planes, sky, halo, params, disp, jac, disp_buf, jac_buf, out_sem):
    rows = sky.shape[1]
    blocks = sky.shape[2] // LANES
    total = blocks + 1
    lane = lax.broadcasted_iota(jnp.int32, (GROUP, LANES), 1)
    row = lax.broadcasted_iota(jnp.int32, (GROUP, LANES), 0)

    def right(parts):
        turned = [pltpu.roll(part, LANES - 1, 1) for part in parts]
        return [
            jnp.where(lane == LANES - 1, turned[(v + 1) % total], turned[v])
            for v in range(total)
        ]

    def left(parts):
        turned = [pltpu.roll(part, 1, 1) for part in parts]
        return [jnp.where(lane == 0, turned[v - 1], turned[v]) for v in range(total)]

    def load(k, start, stop):
        parts = [sky[k, start:stop, v * LANES : (v + 1) * LANES] for v in range(blocks)]
        return parts + [halo[k, start:stop, :]]

    copies = []
    for g in range(rows // GROUP):
        start, stop = g * GROUP, (g + 1) * GROUP
        column = [
            jnp.broadcast_to(params[start:stop, i : i + 1], (GROUP, LANES))
            for i in range(5 + planes)
        ]
        metric = column[4]
        stencils = []
        for side in range(2):
            place = lane + column[side].astype(jnp.int32)
            frac = column[2 + side]
            stencils.append((place & (LANES - 1), place < 0, place >= LANES, frac, 1.0 - frac))
        state = [None] * blocks
        for k in range(planes):
            gain = column[5 + k]
            here = load(k, start, stop)
            if g == 0:
                above = [jnp.where(row == 0, 0.0, pltpu.roll(part, 1, 0)) for part in here]
            else:
                above = load(k, start - 1, stop - 1)
            if stop == rows:
                below = [
                    jnp.where(row == GROUP - 1, 0.0, pltpu.roll(part, GROUP - 1, 0))
                    for part in here
                ]
            else:
                below = load(k, start + 1, stop + 1)
            values = []
            for (place, under, over, frac, rest), parts in zip(stencils, (above, below)):
                mixed = [rest * a + frac * b for a, b in zip(parts, right(parts))]
                picked = [jnp.take_along_axis(part, place, axis=1) for part in mixed]
                values.append(
                    [
                        jnp.where(
                            under,
                            picked[v - 1],
                            jnp.where(over, picked[(v + 1) % total], picked[v]),
                        )
                        for v in range(total)
                    ]
                )
            north, south = values
            slope = [s - n for s, n in zip(south, north)]
            slope_right, slope_left = right(slope), left(slope)
            here_right, here_left = right(here), left(here)
            for v in range(blocks):
                alpha_t = 0.5 * slope[v]
                alpha_p = 0.5 * metric * (here_right[v] - here_left[v])
                u_tt = south[v] - 2.0 * here[v] + north[v]
                u_pp = metric * metric * (here_right[v] - 2.0 * here[v] + here_left[v])
                u_tp = 0.25 * metric * (slope_right[v] - slope_left[v])
                if k == 0:
                    off = -gain * u_tp
                    state[v] = (
                        -gain * alpha_t, -gain * alpha_p,
                        1.0 - gain * u_tt, off, off, 1.0 - gain * u_pp,
                    )
                else:
                    d_t, d_p, zz, zo, oz, oo = state[v]
                    state[v] = (
                        d_t - gain * (alpha_t + u_tt * d_t + u_tp * d_p),
                        d_p - gain * (alpha_p + u_tp * d_t + u_pp * d_p),
                        zz - gain * (u_tt * zz + u_tp * oz),
                        zo - gain * (u_tt * zo + u_tp * oo),
                        oz - gain * (u_tp * zz + u_pp * oz),
                        oo - gain * (u_tp * zo + u_pp * oo),
                    )
        for v in range(blocks):
            part = pl.ds(v * LANES, LANES)
            for i in range(2):
                disp_buf[i, start:stop, part] = state[v][i]
            for i in range(4):
                jac_buf[i, start:stop, part] = state[v][2 + i]
        here = pl.ds(start, GROUP)
        for i, (source, target) in enumerate(((disp_buf, disp), (jac_buf, jac))):
            copy = pltpu.make_async_copy(
                source.at[:, here], target.at[0, :, here], out_sem.at[i, g]
            )
            copy.start()
            copies.append(copy)
    for copy in copies:
        copy.wait()


def per_device(planes, count, potential, lens_weight, cycle_shift, cycle_weight, cycle_scale):
    rows, width = potential.shape[1:]
    f32 = jnp.float32
    vmem = pl.BlockSpec(memory_space=pltpu.VMEM)
    anywhere = pl.BlockSpec(memory_space=pl.ANY)
    hbm = pl.BlockSpec(memory_space=pltpu.HBM)
    dma = pltpu.SemaphoreType.DMA
    sky, halo, params = pl.pallas_call(
        functools.partial(exchange_kernel, planes, count, count // 4),
        out_shape=(
            jax.ShapeDtypeStruct((planes, rows, width), f32),
            jax.ShapeDtypeStruct((planes, rows, LANES), f32),
            jax.ShapeDtypeStruct((rows, LANES), f32),
        ),
        in_specs=[hbm] * 5,
        out_specs=(vmem, vmem, vmem),
        scratch_shapes=[
            pltpu.VMEM((rows, width), f32),
            pltpu.SMEM((1, planes), f32),
            pltpu.VMEM((2, rows), jnp.int32),
            pltpu.VMEM((2, rows), jnp.int32),
            pltpu.VMEM((rows,), f32),
            pltpu.VMEM((PACK, rows), f32),
            pltpu.VMEM((PACK, rows), f32),
            pltpu.VMEM((planes, LANES, rows), f32),
            pltpu.VMEM((LANES, rows), f32),
            dma((5,)),
            dma((CHUNKS,)),
            dma((CHUNKS,)),
            dma((planes - 1, CHUNKS)),
            dma((planes, CHUNKS)),
            dma((planes, 2)),
            dma((planes, 2)),
        ],
        compiler_params=pltpu.CompilerParams(
            collective_id=0, has_side_effects=True, vmem_limit_bytes=32 * 2**20
        ),
        name="exchange",
    )(potential, lens_weight, cycle_shift, cycle_weight, cycle_scale)
    return tuple(
        pl.pallas_call(
            functools.partial(ray_kernel, planes),
            out_shape=(
                jax.ShapeDtypeStruct((1, 2, rows, width), f32),
                jax.ShapeDtypeStruct((1, 4, rows, width), f32),
            ),
            in_specs=[vmem, vmem, vmem],
            out_specs=(anywhere, anywhere),
            scratch_shapes=[
                pltpu.VMEM((2, rows, width), f32),
                pltpu.VMEM((4, rows, width), f32),
                dma((2, rows // GROUP)),
            ],
            compiler_params=pltpu.CompilerParams(vmem_limit_bytes=32 * 2**20),
            name="rays",
        )(sky, halo, params)
    )


def solution(mesh):
    in_specs = (P("plane", None, "lon"), P("plane", None), P(), P(), P())
    out_specs = (P("plane", None, None, "lon"), P("plane", None, None, "lon"))
    return jax.shard_map(
        functools.partial(per_device, mesh.shape["plane"], mesh.shape["lon"]),
        mesh=mesh, in_specs=in_specs, out_specs=out_specs, check_vma=False,
    )
```

```python
import functools

import jax
import jax.numpy as jnp
from jax import lax
from jax.experimental import pallas as pl
from jax.experimental.pallas import tpu as pltpu
from jax.sharding import PartitionSpec as P

LANES = 128
PACK = 8
CHUNKS = 8
LAG = 2


def lens_kernel(
    planes, count, turn,
    pot, gains_hbm, shift_hbm, weight_hbm, scale_hbm,
    disp, jac,
    sky, halo, params, fields, disp_buf, jac_buf, tile, gains, shift, weight, scale, low_pack, high_pack, strips, columns,
    load_sem, turn_send, turn_recv, plane_send, plane_recv, halo_send, halo_recv, out_sem,
):
    me = lax.axis_index("lon")
    own = lax.axis_index("plane")
    rows = pot.shape[1]
    step = rows // CHUNKS

    def at(moves, plane):
        return {"lon": lax.rem(me + moves + count, count), "plane": plane}

    others = [lax.rem(own + d, planes) for d in range(1, planes)]
    loads = [
        pltpu.make_async_copy(source, target, load_sem.at[i])
        for i, (source, target) in enumerate(
            (
                (pot.at[0], tile), (gains_hbm, gains), (shift_hbm, shift),
                (weight_hbm, weight), (scale_hbm, scale),
            )
        )
    ]
    for load in loads:
        load.start()

    barrier = pltpu.get_barrier_semaphore()
    senders = [at(turn, own)] + [at(0, q) for q in others]
    senders += [at(turn + side, q) for side in (-1, 1) for q in [own] + others]
    for device in senders:
        pl.semaphore_signal(
            barrier, inc=1, device_id=device, device_id_type=pl.DeviceIdType.MESH
        )
    pl.semaphore_wait(barrier, len(senders))

    turned = []
    for k in range(CHUNKS):
        part = pl.ds(k * step, step)
        copy = pltpu.make_async_remote_copy(
            src_ref=pot.at[0, part],
            dst_ref=sky.at[own, part],
            send_sem=turn_send.at[k],
            recv_sem=turn_recv.at[k],
            device_id=at(-turn, own),
            device_id_type=pl.DeviceIdType.MESH,
        )
        copy.start()
        turned.append(copy)

    for load in loads:
        load.wait()
    low_pack[...] = jnp.transpose(tile[:, :LANES])[:PACK]
    high_pack[...] = jnp.transpose(tile[:, tile.shape[1] - LANES :])[LANES - PACK :]
    edges = []
    for i, q in enumerate([own] + others):
        for side, (source, first, moves) in enumerate(
            ((low_pack, 0, -turn - 1), (high_pack, LANES - PACK, -turn + 1))
        ):
            copy = pltpu.make_async_remote_copy(
                src_ref=source,
                dst_ref=strips.at[own, pl.ds(first, PACK)],
                send_sem=halo_send.at[i, side],
                recv_sem=halo_recv.at[own, side],
                device_id=at(moves, q),
                device_id_type=pl.DeviceIdType.MESH,
            )
            copy.start()
            edges.append(copy)

    columns[...] = jnp.zeros_like(columns)
    columns[0:2] = shift[...].astype(jnp.float32)
    columns[2:4] = weight[...].astype(jnp.float32) / 16.0
    columns[4:5] = scale[...].reshape(1, rows)
    params[...] = jnp.transpose(columns[...])
    strips[:, PACK : LANES - PACK] = jnp.zeros(
        (planes, LANES - 2 * PACK, rows), jnp.float32
    )

    lane = lax.broadcasted_iota(jnp.int32, (step, LANES), 1)
    row = lax.broadcasted_iota(jnp.int32, (step, LANES), 0)
    blocks = sky.shape[2] // LANES
    total = blocks + 1

    def right(parts):
        turns = [pltpu.roll(part, LANES - 1, 1) for part in parts]
        return [
            jnp.where(lane == LANES - 1, turns[(v + 1) % total], turns[v])
            for v in range(total)
        ]

    def left(parts):
        turns = [pltpu.roll(part, 1, 1) for part in parts]
        return [jnp.where(lane == 0, turns[v - 1], turns[v]) for v in range(total)]

    def column(g, i):
        return jnp.broadcast_to(params[g * step : (g + 1) * step, i : i + 1], (step, LANES))

    def load(k, start, stop):
        parts = [sky[k, start:stop, v * LANES : (v + 1) * LANES] for v in range(blocks)]
        return parts + [halo[k, start:stop, :]]

    def derive(k, g):
        start, stop = g * step, (g + 1) * step
        metric = column(g, 4)
        here = load(k, start, stop)
        if g == 0:
            above = [jnp.where(row == 0, 0.0, pltpu.roll(part, 1, 0)) for part in here]
        else:
            above = load(k, start - 1, stop - 1)
        if stop == rows:
            below = [jnp.where(row == step - 1, 0.0, pltpu.roll(part, step - 1, 0)) for part in here]
        else:
            below = load(k, start + 1, stop + 1)
        values = []
        for side, parts in enumerate((above, below)):
            spot = lane + column(g, side).astype(jnp.int32)
            place = spot & (LANES - 1)
            under, over = spot < 0, spot >= LANES
            frac = column(g, 2 + side)
            rest = 1.0 - frac
            mixed = [rest * a + frac * b for a, b in zip(parts, right(parts))]
            picked = [jnp.take_along_axis(part, place, axis=1) for part in mixed]
            values.append(
                [
                    jnp.where(
                        under,
                        picked[v - 1],
                        jnp.where(over, picked[(v + 1) % total], picked[v]),
                    )
                    for v in range(total)
                ]
            )
        north, south = values
        slope = [s - n for s, n in zip(south, north)]
        slope_right, slope_left = right(slope), left(slope)
        here_right, here_left = right(here), left(here)
        for v in range(blocks):
            found = (
                0.5 * slope[v],
                0.5 * metric * (here_right[v] - here_left[v]),
                south[v] - 2.0 * here[v] + north[v],
                metric * metric * (here_right[v] - 2.0 * here[v] + here_left[v]),
                0.25 * metric * (slope_right[v] - slope_left[v]),
            )
            for i, field in enumerate(found):
                fields[k, i, start:stop, v * LANES : (v + 1) * LANES] = field

    written = []

    def trace(g):
        start, stop = g * step, (g + 1) * step
        for v in range(blocks):
            part = slice(v * LANES, (v + 1) * LANES)
            for k in range(planes):
                gain = gains[0, k]
                alpha_t, alpha_p, u_tt, u_pp, u_tp = [
                    fields[k, i, start:stop, part] for i in range(5)
                ]
                if k == 0:
                    off = -gain * u_tp
                    d_t, d_p = -gain * alpha_t, -gain * alpha_p
                    zz, zo, oz, oo = 1.0 - gain * u_tt, off, off, 1.0 - gain * u_pp
                else:
                    d_t, d_p, zz, zo, oz, oo = (
                        d_t - gain * (alpha_t + u_tt * d_t + u_tp * d_p),
                        d_p - gain * (alpha_p + u_tp * d_t + u_pp * d_p),
                        zz - gain * (u_tt * zz + u_tp * oz),
                        zo - gain * (u_tt * zo + u_tp * oo),
                        oz - gain * (u_tp * zz + u_pp * oz),
                        oo - gain * (u_tp * zo + u_pp * oo),
                    )
            for i, value in enumerate((d_t, d_p)):
                disp_buf[i, start:stop, part] = value
            for i, value in enumerate((zz, zo, oz, oo)):
                jac_buf[i, start:stop, part] = value
        for i, (source, target) in enumerate(((disp_buf, disp), (jac_buf, jac))):
            copy = pltpu.make_async_copy(
                source.at[:, pl.ds(start, step)],
                target.at[0, :, pl.ds(start, step)],
                out_sem.at[i, g],
            )
            copy.start()
            written.append(copy)

    def edges_arrive(q):
        for side, (source, first) in enumerate(((low_pack, 0), (high_pack, LANES - PACK))):
            pltpu.make_async_remote_copy(
                src_ref=source,
                dst_ref=strips.at[q, pl.ds(first, PACK)],
                send_sem=halo_send.at[0, side],
                recv_sem=halo_recv.at[q, side],
                device_id=at(0, others[0]),
                device_id_type=pl.DeviceIdType.MESH,
            ).wait_recv()
        halo[q] = jnp.transpose(strips[q])

    handed = []
    for k in range(CHUNKS + 1 + LAG):
        if k < CHUNKS:
            part = pl.ds(k * step, step)
            turned[k].wait_recv()
            for i, q in enumerate(others):
                copy = pltpu.make_async_remote_copy(
                    src_ref=sky.at[own, part],
                    dst_ref=sky.at[own, part],
                    send_sem=plane_send.at[i, k],
                    recv_sem=plane_recv.at[own, k],
                    device_id=at(0, q),
                    device_id_type=pl.DeviceIdType.MESH,
                )
                copy.start()
                handed.append(copy)
        if k == 0:
            edges_arrive(own)
        if 1 <= k <= CHUNKS:
            derive(own, k - 1)
        late = k - LAG
        if 0 <= late < CHUNKS:
            for q in others:
                part = pl.ds(late * step, step)
                pltpu.make_async_remote_copy(
                    src_ref=sky.at[q, part],
                    dst_ref=sky.at[q, part],
                    send_sem=plane_send.at[0, late],
                    recv_sem=plane_recv.at[q, late],
                    device_id=at(0, others[0]),
                    device_id_type=pl.DeviceIdType.MESH,
                ).wait_recv()
                if late == 0:
                    edges_arrive(q)
        if 1 <= late:
            for q in others:
                derive(q, late - 1)
            trace(late - 1)
    for copy in turned + edges + handed:
        copy.wait_send()
    for copy in written:
        copy.wait()


def per_device(planes, count, potential, lens_weight, cycle_shift, cycle_weight, cycle_scale):
    rows, width = potential.shape[1:]
    f32 = jnp.float32
    anywhere = pl.BlockSpec(memory_space=pl.ANY)
    dma = pltpu.SemaphoreType.DMA
    return tuple(
        pl.pallas_call(
            functools.partial(lens_kernel, planes, count, count // 4),
            out_shape=(
                jax.ShapeDtypeStruct((1, 2, rows, width), f32),
                jax.ShapeDtypeStruct((1, 4, rows, width), f32),
            ),
            in_specs=[anywhere] * 5,
            out_specs=(anywhere, anywhere),
            scratch_shapes=[
                pltpu.VMEM((planes, rows, width), f32),
                pltpu.VMEM((planes, rows, LANES), f32),
                pltpu.VMEM((rows, LANES), f32),
                pltpu.VMEM((planes, 5, rows, width), f32),
                pltpu.VMEM((2, rows, width), f32),
                pltpu.VMEM((4, rows, width), f32),
                pltpu.VMEM((rows, width), f32),
                pltpu.SMEM((1, planes), f32),
                pltpu.VMEM((2, rows), jnp.int32),
                pltpu.VMEM((2, rows), jnp.int32),
                pltpu.VMEM((rows,), f32),
                pltpu.VMEM((PACK, rows), f32),
                pltpu.VMEM((PACK, rows), f32),
                pltpu.VMEM((planes, LANES, rows), f32),
                pltpu.VMEM((LANES, rows), f32),
                dma((5,)),
                dma((CHUNKS,)),
                dma((CHUNKS,)),
                dma((planes - 1, CHUNKS)),
                dma((planes, CHUNKS)),
                dma((planes, 2)),
                dma((planes, 2)),
                dma((2, CHUNKS)),
            ],
            compiler_params=pltpu.CompilerParams(
                collective_id=0, has_side_effects=True, vmem_limit_bytes=60 * 2**20
            ),
            name="lens",
        )(potential, lens_weight, cycle_shift, cycle_weight, cycle_scale)
    )


def solution(mesh):
    in_specs = (P("plane", None, "lon"), P("plane", None), P(), P(), P())
    out_specs = (P("plane", None, None, "lon"), P("plane", None, None, "lon"))
    return jax.shard_map(
        functools.partial(per_device, mesh.shape["plane"], mesh.shape["lon"]),
        mesh=mesh, in_specs=in_specs, out_specs=out_specs, check_vma=False,
    )
```

```python
import functools

import jax
import jax.numpy as jnp
from jax import lax
from jax.experimental import pallas as pl
from jax.experimental.pallas import tpu as pltpu
from jax.sharding import PartitionSpec as P

LANES = 128
PACK = 8
CHUNKS = 4
LAG = 2


def lens_kernel(
    planes, count, turn,
    pot, gains_hbm, shift_hbm, weight_hbm, scale_hbm,
    disp, jac,
    sky, halo, params, fields, disp_buf, jac_buf, tile, gains, shift, weight, scale, low_pack, high_pack, strips, columns,
    load_sem, turn_send, turn_recv, plane_send, plane_recv, halo_send, halo_recv, out_sem,
):
    me = lax.axis_index("lon")
    own = lax.axis_index("plane")
    rows = pot.shape[1]
    step = rows // CHUNKS

    def at(moves, plane):
        return {"lon": lax.rem(me + moves + count, count), "plane": plane}

    others = [lax.rem(own + d, planes) for d in range(1, planes)]
    loads = [
        pltpu.make_async_copy(source, target, load_sem.at[i])
        for i, (source, target) in enumerate(
            (
                (pot.at[0], tile), (gains_hbm, gains), (shift_hbm, shift),
                (weight_hbm, weight), (scale_hbm, scale),
            )
        )
    ]
    for load in loads:
        load.start()

    barrier = pltpu.get_barrier_semaphore()
    senders = [at(turn, own)] + [at(0, q) for q in others]
    senders += [at(turn + side, q) for side in (-1, 1) for q in [own] + others]
    for device in senders:
        pl.semaphore_signal(
            barrier, inc=1, device_id=device, device_id_type=pl.DeviceIdType.MESH
        )
    pl.semaphore_wait(barrier, len(senders))

    turned = []
    for k in range(CHUNKS):
        part = pl.ds(k * step, step)
        copy = pltpu.make_async_remote_copy(
            src_ref=pot.at[0, part],
            dst_ref=sky.at[own, part],
            send_sem=turn_send.at[k],
            recv_sem=turn_recv.at[k],
            device_id=at(-turn, own),
            device_id_type=pl.DeviceIdType.MESH,
        )
        turned.append(copy)
    for copy in turned[: CHUNKS // 2]:
        copy.start()

    for load in loads:
        load.wait()
    low_pack[...] = jnp.transpose(tile[:, :LANES])[:PACK]
    high_pack[...] = jnp.transpose(tile[:, tile.shape[1] - LANES :])[LANES - PACK :]
    edges = []
    for i, q in enumerate([own] + others):
        for side, (source, first, moves) in enumerate(
            ((low_pack, 0, -turn - 1), (high_pack, LANES - PACK, -turn + 1))
        ):
            copy = pltpu.make_async_remote_copy(
                src_ref=source,
                dst_ref=strips.at[own, pl.ds(first, PACK)],
                send_sem=halo_send.at[i, side],
                recv_sem=halo_recv.at[own, side],
                device_id=at(moves, q),
                device_id_type=pl.DeviceIdType.MESH,
            )
            copy.start()
            edges.append(copy)
    turned[CHUNKS // 2].start()

    columns[...] = jnp.zeros_like(columns)
    columns[0:2] = shift[...].astype(jnp.float32)
    columns[2:4] = weight[...].astype(jnp.float32) / 16.0
    columns[4:5] = scale[...].reshape(1, rows)
    params[...] = jnp.transpose(columns[...])
    strips[:, PACK : LANES - PACK] = jnp.zeros(
        (planes, LANES - 2 * PACK, rows), jnp.float32
    )

    for copy in turned[CHUNKS // 2 + 1 :]:
        copy.start()
    lane = lax.broadcasted_iota(jnp.int32, (step, LANES), 1)
    row = lax.broadcasted_iota(jnp.int32, (step, LANES), 0)
    blocks = sky.shape[2] // LANES
    total = blocks + 1

    def right(parts):
        turns = [pltpu.roll(part, LANES - 1, 1) for part in parts]
        return [
            jnp.where(lane == LANES - 1, turns[(v + 1) % total], turns[v])
            for v in range(total)
        ]

    def left(parts):
        turns = [pltpu.roll(part, 1, 1) for part in parts]
        return [jnp.where(lane == 0, turns[v - 1], turns[v]) for v in range(total)]

    def column(g, i):
        return jnp.broadcast_to(params[g * step : (g + 1) * step, i : i + 1], (step, LANES))

    def load(k, start, stop):
        parts = [sky[k, start:stop, v * LANES : (v + 1) * LANES] for v in range(blocks)]
        return parts + [halo[k, start:stop, :]]

    def derive(k, g):
        start, stop = g * step, (g + 1) * step
        metric = column(g, 4)
        here = load(k, start, stop)
        if g == 0:
            above = [jnp.where(row == 0, 0.0, pltpu.roll(part, 1, 0)) for part in here]
        else:
            above = load(k, start - 1, stop - 1)
        if stop == rows:
            below = [jnp.where(row == step - 1, 0.0, pltpu.roll(part, step - 1, 0)) for part in here]
        else:
            below = load(k, start + 1, stop + 1)
        values = []
        for side, parts in enumerate((above, below)):
            spot = lane + column(g, side).astype(jnp.int32)
            place = spot & (LANES - 1)
            under, over = spot < 0, spot >= LANES
            frac = column(g, 2 + side)
            rest = 1.0 - frac
            mixed = [rest * a + frac * b for a, b in zip(parts, right(parts))]
            picked = [jnp.take_along_axis(part, place, axis=1) for part in mixed]
            values.append(
                [
                    jnp.where(
                        under,
                        picked[v - 1],
                        jnp.where(over, picked[(v + 1) % total], picked[v]),
                    )
                    for v in range(total)
                ]
            )
        north, south = values
        slope = [s - n for s, n in zip(south, north)]
        slope_right, slope_left = right(slope), left(slope)
        here_right, here_left = right(here), left(here)
        for v in range(blocks):
            found = (
                0.5 * slope[v],
                0.5 * metric * (here_right[v] - here_left[v]),
                south[v] - 2.0 * here[v] + north[v],
                metric * metric * (here_right[v] - 2.0 * here[v] + here_left[v]),
                0.25 * metric * (slope_right[v] - slope_left[v]),
            )
            for i, field in enumerate(found):
                fields[k, i, start:stop, v * LANES : (v + 1) * LANES] = field

    written = []

    def trace(g):
        start, stop = g * step, (g + 1) * step
        for v in range(blocks):
            part = slice(v * LANES, (v + 1) * LANES)
            for k in range(planes):
                gain = gains[0, k]
                alpha_t, alpha_p, u_tt, u_pp, u_tp = [
                    fields[k, i, start:stop, part] for i in range(5)
                ]
                if k == 0:
                    off = -gain * u_tp
                    d_t, d_p = -gain * alpha_t, -gain * alpha_p
                    zz, zo, oz, oo = 1.0 - gain * u_tt, off, off, 1.0 - gain * u_pp
                else:
                    d_t, d_p, zz, zo, oz, oo = (
                        d_t - gain * (alpha_t + u_tt * d_t + u_tp * d_p),
                        d_p - gain * (alpha_p + u_tp * d_t + u_pp * d_p),
                        zz - gain * (u_tt * zz + u_tp * oz),
                        zo - gain * (u_tt * zo + u_tp * oo),
                        oz - gain * (u_tp * zz + u_pp * oz),
                        oo - gain * (u_tp * zo + u_pp * oo),
                    )
            for i, value in enumerate((d_t, d_p)):
                disp_buf[i, start:stop, part] = value
            for i, value in enumerate((zz, zo, oz, oo)):
                jac_buf[i, start:stop, part] = value
        for i, (source, target) in enumerate(((disp_buf, disp), (jac_buf, jac))):
            copy = pltpu.make_async_copy(
                source.at[:, pl.ds(start, step)],
                target.at[0, :, pl.ds(start, step)],
                out_sem.at[i, g],
            )
            copy.start()
            written.append(copy)

    def edges_arrive(q):
        for side, (source, first) in enumerate(((low_pack, 0), (high_pack, LANES - PACK))):
            pltpu.make_async_remote_copy(
                src_ref=source,
                dst_ref=strips.at[q, pl.ds(first, PACK)],
                send_sem=halo_send.at[0, side],
                recv_sem=halo_recv.at[q, side],
                device_id=at(0, others[0]),
                device_id_type=pl.DeviceIdType.MESH,
            ).wait_recv()
        halo[q] = jnp.transpose(strips[q])

    handed = []
    for k in range(CHUNKS + 1 + LAG):
        if k < CHUNKS:
            part = pl.ds(k * step, step)
            turned[k].wait_recv()
            for i, q in enumerate(others):
                copy = pltpu.make_async_remote_copy(
                    src_ref=sky.at[own, part],
                    dst_ref=sky.at[own, part],
                    send_sem=plane_send.at[i, k],
                    recv_sem=plane_recv.at[own, k],
                    device_id=at(0, q),
                    device_id_type=pl.DeviceIdType.MESH,
                )
                copy.start()
                handed.append(copy)
        if k == 0:
            edges_arrive(own)
        if 1 <= k <= CHUNKS:
            derive(own, k - 1)
        late = k - LAG
        if 0 <= late < CHUNKS:
            for q in others:
                part = pl.ds(late * step, step)
                pltpu.make_async_remote_copy(
                    src_ref=sky.at[q, part],
                    dst_ref=sky.at[q, part],
                    send_sem=plane_send.at[0, late],
                    recv_sem=plane_recv.at[q, late],
                    device_id=at(0, others[0]),
                    device_id_type=pl.DeviceIdType.MESH,
                ).wait_recv()
                if late == 0:
                    edges_arrive(q)
        if 1 <= late:
            for q in others:
                derive(q, late - 1)
            trace(late - 1)
    for copy in turned + edges + handed:
        copy.wait_send()
    for copy in written:
        copy.wait()


def per_device(planes, count, potential, lens_weight, cycle_shift, cycle_weight, cycle_scale):
    rows, width = potential.shape[1:]
    f32 = jnp.float32
    anywhere = pl.BlockSpec(memory_space=pl.ANY)
    dma = pltpu.SemaphoreType.DMA
    return tuple(
        pl.pallas_call(
            functools.partial(lens_kernel, planes, count, count // 4),
            out_shape=(
                jax.ShapeDtypeStruct((1, 2, rows, width), f32),
                jax.ShapeDtypeStruct((1, 4, rows, width), f32),
            ),
            in_specs=[anywhere] * 5,
            out_specs=(anywhere, anywhere),
            scratch_shapes=[
                pltpu.VMEM((planes, rows, width), f32),
                pltpu.VMEM((planes, rows, LANES), f32),
                pltpu.VMEM((rows, LANES), f32),
                pltpu.VMEM((planes, 5, rows, width), f32),
                pltpu.VMEM((2, rows, width), f32),
                pltpu.VMEM((4, rows, width), f32),
                pltpu.VMEM((rows, width), f32),
                pltpu.SMEM((1, planes), f32),
                pltpu.VMEM((2, rows), jnp.int32),
                pltpu.VMEM((2, rows), jnp.int32),
                pltpu.VMEM((rows,), f32),
                pltpu.VMEM((PACK, rows), f32),
                pltpu.VMEM((PACK, rows), f32),
                pltpu.VMEM((planes, LANES, rows), f32),
                pltpu.VMEM((LANES, rows), f32),
                dma((5,)),
                dma((CHUNKS,)),
                dma((CHUNKS,)),
                dma((planes - 1, CHUNKS)),
                dma((planes, CHUNKS)),
                dma((planes, 2)),
                dma((planes, 2)),
                dma((2, CHUNKS)),
            ],
            compiler_params=pltpu.CompilerParams(
                collective_id=0, has_side_effects=True, vmem_limit_bytes=60 * 2**20
            ),
            name="lens",
        )(potential, lens_weight, cycle_shift, cycle_weight, cycle_scale)
    )


def solution(mesh):
    in_specs = (P("plane", None, "lon"), P("plane", None), P(), P(), P())
    out_specs = (P("plane", None, None, "lon"), P("plane", None, None, "lon"))
    return jax.shard_map(
        functools.partial(per_device, mesh.shape["plane"], mesh.shape["lon"]),
        mesh=mesh, in_specs=in_specs, out_specs=out_specs, check_vma=False,
    )
```

```python
import functools

import jax
import jax.numpy as jnp
from jax import lax
from jax.experimental import pallas as pl
from jax.experimental.pallas import tpu as pltpu
from jax.sharding import PartitionSpec as P

LANES = 128
PACK = 8
CHUNKS = 4
LAG = 3


def lens_kernel(
    planes, count, turn,
    pot, gains_hbm, shift_hbm, weight_hbm, scale_hbm,
    disp, jac,
    sky, halo, params, fields, disp_buf, jac_buf, tile, gains, shift, weight, scale, low_pack, high_pack, strips, columns,
    load_sem, turn_send, turn_recv, plane_send, plane_recv, halo_send, halo_recv, out_sem,
):
    me = lax.axis_index("lon")
    own = lax.axis_index("plane")
    rows = pot.shape[1]
    step = rows // CHUNKS

    def at(moves, plane):
        return {"lon": lax.rem(me + moves + count, count), "plane": plane}

    others = [lax.rem(own + d, planes) for d in range(1, planes)]
    loads = [
        pltpu.make_async_copy(source, target, load_sem.at[i])
        for i, (source, target) in enumerate(
            (
                (pot.at[0], tile), (gains_hbm, gains), (shift_hbm, shift),
                (weight_hbm, weight), (scale_hbm, scale),
            )
        )
    ]
    for load in loads:
        load.start()

    barrier = pltpu.get_barrier_semaphore()
    senders = [at(turn, own)] + [at(0, q) for q in others]
    senders += [at(turn + side, q) for side in (-1, 1) for q in [own] + others]
    for device in senders:
        pl.semaphore_signal(
            barrier, inc=1, device_id=device, device_id_type=pl.DeviceIdType.MESH
        )
    pl.semaphore_wait(barrier, len(senders))

    turned = []
    for k in range(CHUNKS):
        part = pl.ds(k * step, step)
        copy = pltpu.make_async_remote_copy(
            src_ref=pot.at[0, part],
            dst_ref=sky.at[own, part],
            send_sem=turn_send.at[k],
            recv_sem=turn_recv.at[k],
            device_id=at(-turn, own),
            device_id_type=pl.DeviceIdType.MESH,
        )
        turned.append(copy)
    for copy in turned[: CHUNKS // 2]:
        copy.start()

    for load in loads:
        load.wait()
    low_pack[...] = jnp.transpose(tile[:, :LANES])[:PACK]
    high_pack[...] = jnp.transpose(tile[:, tile.shape[1] - LANES :])[LANES - PACK :]
    edges = []
    for i, q in enumerate([own] + others):
        for side, (source, first, moves) in enumerate(
            ((low_pack, 0, -turn - 1), (high_pack, LANES - PACK, -turn + 1))
        ):
            copy = pltpu.make_async_remote_copy(
                src_ref=source,
                dst_ref=strips.at[own, pl.ds(first, PACK)],
                send_sem=halo_send.at[i, side],
                recv_sem=halo_recv.at[own, side],
                device_id=at(moves, q),
                device_id_type=pl.DeviceIdType.MESH,
            )
            copy.start()
            edges.append(copy)
    turned[CHUNKS // 2].start()

    columns[...] = jnp.zeros_like(columns)
    columns[0:2] = shift[...].astype(jnp.float32)
    columns[2:4] = weight[...].astype(jnp.float32) / 16.0
    columns[4:5] = scale[...].reshape(1, rows)
    params[...] = jnp.transpose(columns[...])
    strips[:, PACK : LANES - PACK] = jnp.zeros(
        (planes, LANES - 2 * PACK, rows), jnp.float32
    )

    for copy in turned[CHUNKS // 2 + 1 :]:
        copy.start()
    lane = lax.broadcasted_iota(jnp.int32, (step, LANES), 1)
    row = lax.broadcasted_iota(jnp.int32, (step, LANES), 0)
    blocks = sky.shape[2] // LANES
    total = blocks + 1

    def right(parts):
        turns = [pltpu.roll(part, LANES - 1, 1) for part in parts]
        return [
            jnp.where(lane == LANES - 1, turns[(v + 1) % total], turns[v])
            for v in range(total)
        ]

    def left(parts):
        turns = [pltpu.roll(part, 1, 1) for part in parts]
        return [jnp.where(lane == 0, turns[v - 1], turns[v]) for v in range(total)]

    def column(g, i):
        return jnp.broadcast_to(params[g * step : (g + 1) * step, i : i + 1], (step, LANES))

    def load(k, start, stop):
        parts = [sky[k, start:stop, v * LANES : (v + 1) * LANES] for v in range(blocks)]
        return parts + [halo[k, start:stop, :]]

    def derive(k, g):
        start, stop = g * step, (g + 1) * step
        metric = column(g, 4)
        here = load(k, start, stop)
        if g == 0:
            above = [jnp.where(row == 0, 0.0, pltpu.roll(part, 1, 0)) for part in here]
        else:
            above = load(k, start - 1, stop - 1)
        if stop == rows:
            below = [jnp.where(row == step - 1, 0.0, pltpu.roll(part, step - 1, 0)) for part in here]
        else:
            below = load(k, start + 1, stop + 1)
        values = []
        for side, parts in enumerate((above, below)):
            spot = lane + column(g, side).astype(jnp.int32)
            place = spot & (LANES - 1)
            under, over = spot < 0, spot >= LANES
            frac = column(g, 2 + side)
            rest = 1.0 - frac
            mixed = [rest * a + frac * b for a, b in zip(parts, right(parts))]
            picked = [jnp.take_along_axis(part, place, axis=1) for part in mixed]
            values.append(
                [
                    jnp.where(
                        under,
                        picked[v - 1],
                        jnp.where(over, picked[(v + 1) % total], picked[v]),
                    )
                    for v in range(total)
                ]
            )
        north, south = values
        slope = [s - n for s, n in zip(south, north)]
        slope_right, slope_left = right(slope), left(slope)
        here_right, here_left = right(here), left(here)
        for v in range(blocks):
            found = (
                0.5 * slope[v],
                0.5 * metric * (here_right[v] - here_left[v]),
                south[v] - 2.0 * here[v] + north[v],
                metric * metric * (here_right[v] - 2.0 * here[v] + here_left[v]),
                0.25 * metric * (slope_right[v] - slope_left[v]),
            )
            for i, field in enumerate(found):
                fields[k, i, start:stop, v * LANES : (v + 1) * LANES] = field

    written = []

    def trace(g):
        start, stop = g * step, (g + 1) * step
        for v in range(blocks):
            part = slice(v * LANES, (v + 1) * LANES)
            for k in range(planes):
                gain = gains[0, k]
                alpha_t, alpha_p, u_tt, u_pp, u_tp = [
                    fields[k, i, start:stop, part] for i in range(5)
                ]
                if k == 0:
                    off = -gain * u_tp
                    d_t, d_p = -gain * alpha_t, -gain * alpha_p
                    zz, zo, oz, oo = 1.0 - gain * u_tt, off, off, 1.0 - gain * u_pp
                else:
                    d_t, d_p, zz, zo, oz, oo = (
                        d_t - gain * (alpha_t + u_tt * d_t + u_tp * d_p),
                        d_p - gain * (alpha_p + u_tp * d_t + u_pp * d_p),
                        zz - gain * (u_tt * zz + u_tp * oz),
                        zo - gain * (u_tt * zo + u_tp * oo),
                        oz - gain * (u_tp * zz + u_pp * oz),
                        oo - gain * (u_tp * zo + u_pp * oo),
                    )
            for i, value in enumerate((d_t, d_p)):
                disp_buf[i, start:stop, part] = value
            for i, value in enumerate((zz, zo, oz, oo)):
                jac_buf[i, start:stop, part] = value
        for i, (source, target) in enumerate(((disp_buf, disp), (jac_buf, jac))):
            copy = pltpu.make_async_copy(
                source.at[:, pl.ds(start, step)],
                target.at[0, :, pl.ds(start, step)],
                out_sem.at[i, g],
            )
            copy.start()
            written.append(copy)

    def edges_arrive(q):
        for side, (source, first) in enumerate(((low_pack, 0), (high_pack, LANES - PACK))):
            pltpu.make_async_remote_copy(
                src_ref=source,
                dst_ref=strips.at[q, pl.ds(first, PACK)],
                send_sem=halo_send.at[0, side],
                recv_sem=halo_recv.at[q, side],
                device_id=at(0, others[0]),
                device_id_type=pl.DeviceIdType.MESH,
            ).wait_recv()
        halo[q] = jnp.transpose(strips[q])

    handed = []
    for k in range(CHUNKS + 1 + LAG):
        if k < CHUNKS:
            part = pl.ds(k * step, step)
            turned[k].wait_recv()
            for i, q in enumerate(others):
                copy = pltpu.make_async_remote_copy(
                    src_ref=sky.at[own, part],
                    dst_ref=sky.at[own, part],
                    send_sem=plane_send.at[i, k],
                    recv_sem=plane_recv.at[own, k],
                    device_id=at(0, q),
                    device_id_type=pl.DeviceIdType.MESH,
                )
                copy.start()
                handed.append(copy)
        if k == 0:
            edges_arrive(own)
        if 1 <= k <= CHUNKS:
            derive(own, k - 1)
        late = k - LAG
        if 0 <= late < CHUNKS:
            for q in others:
                part = pl.ds(late * step, step)
                pltpu.make_async_remote_copy(
                    src_ref=sky.at[q, part],
                    dst_ref=sky.at[q, part],
                    send_sem=plane_send.at[0, late],
                    recv_sem=plane_recv.at[q, late],
                    device_id=at(0, others[0]),
                    device_id_type=pl.DeviceIdType.MESH,
                ).wait_recv()
                if late == 0:
                    edges_arrive(q)
        if 1 <= late:
            for q in others:
                derive(q, late - 1)
            trace(late - 1)
    for copy in turned + edges + handed:
        copy.wait_send()
    for copy in written:
        copy.wait()


def per_device(planes, count, potential, lens_weight, cycle_shift, cycle_weight, cycle_scale):
    rows, width = potential.shape[1:]
    f32 = jnp.float32
    anywhere = pl.BlockSpec(memory_space=pl.ANY)
    dma = pltpu.SemaphoreType.DMA
    return tuple(
        pl.pallas_call(
            functools.partial(lens_kernel, planes, count, count // 4),
            out_shape=(
                jax.ShapeDtypeStruct((1, 2, rows, width), f32),
                jax.ShapeDtypeStruct((1, 4, rows, width), f32),
            ),
            in_specs=[anywhere] * 5,
            out_specs=(anywhere, anywhere),
            scratch_shapes=[
                pltpu.VMEM((planes, rows, width), f32),
                pltpu.VMEM((planes, rows, LANES), f32),
                pltpu.VMEM((rows, LANES), f32),
                pltpu.VMEM((planes, 5, rows, width), f32),
                pltpu.VMEM((2, rows, width), f32),
                pltpu.VMEM((4, rows, width), f32),
                pltpu.VMEM((rows, width), f32),
                pltpu.SMEM((1, planes), f32),
                pltpu.VMEM((2, rows), jnp.int32),
                pltpu.VMEM((2, rows), jnp.int32),
                pltpu.VMEM((rows,), f32),
                pltpu.VMEM((PACK, rows), f32),
                pltpu.VMEM((PACK, rows), f32),
                pltpu.VMEM((planes, LANES, rows), f32),
                pltpu.VMEM((LANES, rows), f32),
                dma((5,)),
                dma((CHUNKS,)),
                dma((CHUNKS,)),
                dma((planes - 1, CHUNKS)),
                dma((planes, CHUNKS)),
                dma((planes, 2)),
                dma((planes, 2)),
                dma((2, CHUNKS)),
            ],
            compiler_params=pltpu.CompilerParams(
                collective_id=0, has_side_effects=True, vmem_limit_bytes=60 * 2**20
            ),
            name="lens",
        )(potential, lens_weight, cycle_shift, cycle_weight, cycle_scale)
    )


def solution(mesh):
    in_specs = (P("plane", None, "lon"), P("plane", None), P(), P(), P())
    out_specs = (P("plane", None, None, "lon"), P("plane", None, None, "lon"))
    return jax.shard_map(
        functools.partial(per_device, mesh.shape["plane"], mesh.shape["lon"]),
        mesh=mesh, in_specs=in_specs, out_specs=out_specs, check_vma=False,
    )
```
